32 devices in a mesh: dev: 32 (over z, y, x, core).
Axes of the slice: x: 2, y: 2, z: 4, core: 2. Of those that a mesh axis runs over, the one named last changes fastest.
Arguments:
- row_table: float32 [1024, 32, 512], P('dev'), may hold values from -3 to 3
- col_table: float32 [1024, 32, 512], P('dev'), may hold values from -3 to 3
- row_accum: float32 [1024, 32, 512], P('dev'), may hold values from 0.05 to 0.5
- col_accum: float32 [1024, 32, 512], P('dev'), may hold values from 0.05 to 0.5
- row_margin: float32 [1024, 32], P('dev'), may hold values from -2 to 1
- col_margin: float32 [1024, 32], P('dev'), may hold values from -2 to 1
- row_blocks: int32 [64], P('dev'), may hold values from 0 to 31
- col_blocks: int32 [64], P('dev'), may hold values from 0 to 31
- slot_of: int32 [32], replicated, may hold values from 0 to 31, each once
- counts: int32 [64, 1024, 1024], P('dev'), may hold values from 0 to 199, as said below
Outputs:
- new_row_table: float32 [1024, 32, 512], P('dev')
- new_col_table: float32 [1024, 32, 512], P('dev')
- new_row_accum: float32 [1024, 32, 512], P('dev')
- new_col_accum: float32 [1024, 32, 512], P('dev')
The draws below stay inside these ranges and needn't reach their ends.
Inputs may be any that keep to these rules, and one draw needn't show every extreme that they name: `slot_of`: each block appears once. `counts`: about six cells in ten are nonzero.
All inputs are finite; a program needn't handle non-finite values.
Results may differ from the reference program's by a relative error of at most 0.0003.
Values sent between devices are 32-bit elements; how exact they have to be, the bound alone decides.
No kernel may reach another device: no remote copies, remote signals or barrier semaphores. Data moves between devices by JAX's collectives and lax.ppermute only.
A program may use at most 128 MiB of HBM per device.

```python
import math
import jax
import jax.numpy as jnp
import numpy as np
from jax import lax

D = 512
BLK = 1024
NB = 32
SHARDS = 64


def draw_counts(key, part):
    first_key = jax.random.fold_in(key, 11)
    second_key = jax.random.fold_in(key, 23)
    shape = (SHARDS, BLK, BLK)
    values = jax.random.randint(first_key, shape, 1, 200, dtype=jnp.int32)
    keeper = jax.random.randint(second_key, shape, 0, 5, dtype=jnp.int32)
    return jnp.where(keeper >= 2, values, 0).astype(jnp.int32)


def with_ends(values, key, least, top_value):
    longest = values.shape.index(max(values.shape))
    spots = []
    for shift in (0, 1):
        where = [jax.random.randint(jax.random.fold_in(key, axis), (), 0, length) for axis, length in enumerate(values.shape)]
        where[longest] = (where[longest] + shift) % values.shape[longest]
        spots.append(tuple(where))
    return values.at[spots[0]].set(least).at[spots[1]].set(top_value)


def level_of(stream_key, dims, cuts, low, largest):
    gain, own = 1.0, jax.random.fold_in(stream_key, 6)
    for dim, parts in cuts:
        heights = jnp.exp(jax.random.uniform(jax.random.fold_in(own, dim), (parts,), jnp.float32, low / len(cuts), largest / len(cuts)))
        gain = gain * jnp.repeat(heights, dims[dim] // parts).reshape([-1 if axis == dim else 1 for axis in range(len(dims))])
    return gain


def rank_bounds(number_of, skew):
    weights = [(1 << 20) // math.isqrt(standing ** skew) + 1 for standing in range(1, number_of + 1)]
    scale = 1 + sum(weights) // (1 << 30)
    return np.cumsum(np.array([max(1, weight // scale) for weight in weights]))


def ranked(key, dims, amount, slope):
    table = rank_bounds(amount, slope)
    lot = jax.random.randint(jax.random.fold_in(key, 1), dims, 0, int(table[amount - 1]))
    rank = jnp.searchsorted(jnp.asarray(table, jnp.int32), lot, side="right")
    return jax.random.permutation(jax.random.fold_in(key, 2), amount)[rank].astype(jnp.int32)


def noise(key, extent, scale, reach, cuts=(), kind=jnp.bfloat16):
    values = scale * jax.random.normal(key, extent, jnp.float32)
    if cuts:
        values = values * level_of(key, extent, cuts, -0.22, 0.18)
    return jnp.clip(values, -reach, reach).astype(kind)


def setup_inputs(seed: int = 0) -> dict:
    seeds = jax.random.split(jax.random.key(seed), 11)
    return {
        "row_table": noise(seeds[0], (BLK, NB, D), 0.2, 3.0, ((0, 32),), jnp.float32),
        "col_table": noise(seeds[1], (BLK, NB, D), 0.2, 3.0, ((0, 32),), jnp.float32),
        "row_accum": jnp.clip(jnp.exp(math.log(0.5) - 2.3025851 * jax.random.uniform(seeds[2], (BLK, NB, D), jnp.float32) ** level_of(seeds[2], (BLK, NB, D), ((0, 32),), -0.2, 0.2)), 0.05, 0.5),
        "col_accum": jnp.clip(jnp.exp(math.log(0.5) - 2.3025851 * jax.random.uniform(seeds[3], (BLK, NB, D), jnp.float32) ** level_of(seeds[3], (BLK, NB, D), ((0, 32),), -0.2, 0.2)), 0.05, 0.5),
        "row_margin": jnp.clip(-2.0 + 3.0 * jax.random.uniform(seeds[4], (BLK, NB), jnp.float32) ** level_of(seeds[4], (BLK, NB), ((0, 32),), -0.2, 0.2), -2.0, 1.0),
        "col_margin": jnp.clip(-2.0 + 3.0 * jax.random.uniform(seeds[5], (BLK, NB), jnp.float32) ** level_of(seeds[5], (BLK, NB), ((0, 32),), -0.2, 0.2), -2.0, 1.0),
        "row_blocks": with_ends(ranked(seeds[6], (SHARDS,), NB, 2), jax.random.fold_in(seeds[6], 3), 0, NB - 1).astype(jnp.int32),
        "col_blocks": with_ends(ranked(seeds[7], (SHARDS,), NB, 2), jax.random.fold_in(seeds[7], 3), 0, NB - 1).astype(jnp.int32),
        "slot_of": jax.random.permutation(seeds[8], NB).astype(jnp.int32),
        "counts": draw_counts(jax.random.fold_in(seeds[10], 71), 0),
    }


def shard_grads(rows_block, cols_block, margin_r, margin_c, tile_counts):
    high = lax.Precision.HIGHEST
    logits = jnp.dot(rows_block, cols_block.T, precision=high, preferred_element_type=jnp.float32)
    values = tile_counts.astype(jnp.float32)
    target = jnp.log(jnp.maximum(values, 1.0)) - margin_r[:, None] - margin_c[None, :]
    error = logits - target
    confidence = 0.1 + 0.25 * jnp.sqrt(values)
    scaled = jnp.where(tile_counts > 0, confidence * error, jax.nn.sigmoid(error)) / tile_counts.shape[0]
    row_grad = jnp.dot(scaled, cols_block, precision=high, preferred_element_type=jnp.float32)
    col_grad = lax.dot_general(scaled, rows_block, (((0,), (0,)), ((), ())), precision=high, preferred_element_type=jnp.float32)
    return (row_grad, col_grad)

def reference(row_table, col_table, row_accum, col_accum, row_margin, col_margin, row_blocks, col_blocks, slot_of, counts):

    def visit(carry, item):
        grad_rows, grad_cols = carry
        row_id, col_id, tile_counts = item
        row_slot = slot_of[row_id].astype(jnp.int32)
        col_slot = slot_of[col_id].astype(jnp.int32)
        rows_block = lax.dynamic_index_in_dim(row_table, row_slot, 1, keepdims=False)
        cols_block = lax.dynamic_index_in_dim(col_table, col_slot, 1, keepdims=False)
        margin_r = lax.dynamic_index_in_dim(row_margin, row_slot, 1, keepdims=False)
        margin_c = lax.dynamic_index_in_dim(col_margin, col_slot, 1, keepdims=False)
        row_grad, col_grad = shard_grads(rows_block, cols_block, margin_r, margin_c, tile_counts)
        old_rows = lax.dynamic_index_in_dim(grad_rows, row_slot, 1, keepdims=False)
        grad_rows = lax.dynamic_update_index_in_dim(grad_rows, old_rows + row_grad, row_slot, 1)
        old_cols = lax.dynamic_index_in_dim(grad_cols, col_slot, 1, keepdims=False)
        grad_cols = lax.dynamic_update_index_in_dim(grad_cols, old_cols + col_grad, col_slot, 1)
        return ((grad_rows, grad_cols), None)
    zeros = jnp.zeros(row_table.shape, jnp.float32)
    (grad_rows, grad_cols), _ = lax.scan(visit, (zeros, zeros), (row_blocks, col_blocks, counts))
    new_row_accum = row_accum + grad_rows * grad_rows
    new_col_accum = col_accum + grad_cols * grad_cols
    new_row_table = row_table - grad_rows / jnp.sqrt(new_row_accum)
    new_col_table = col_table - grad_cols / jnp.sqrt(new_col_accum)
    return (new_row_table, new_col_table, new_row_accum, new_col_accum)
```

```python
import functools

import jax
import jax.numpy as jnp
from jax import lax
from jax.experimental import pallas as pl
from jax.experimental.pallas import tpu as pltpu
from jax.sharding import PartitionSpec as P

LEAST_GROUP = 32
LANES = 128
VMEM_LIMIT = 56 * 1024 * 1024
F32 = jnp.float32
BF16 = jnp.bfloat16
COST = pl.CostEstimate(flops=1, bytes_accessed=1, transcendentals=0)


def params():
    return pltpu.CompilerParams(vmem_limit_bytes=VMEM_LIMIT)


def lowest_bit(unit):
    return (unit & -unit).bit_length() - 1


def split(x):
    hi = x.astype(BF16)
    return hi, (x - hi.astype(F32)).astype(BF16)


def dot3(a_hi, a_lo, b_hi, b_lo, dims):
    def dot(a, b):
        return lax.dot_general(a, b, (dims, ((), ())), preferred_element_type=F32)

    return dot(a_hi, b_hi) + dot(a_hi, b_lo) + dot(a_lo, b_hi)


def block_major_kernel(row_ref, col_ref, out_ref):
    tiles = pl.num_programs(0) // 2

    @pl.when(pl.program_id(0) < tiles)
    def _():
        out_ref[...] = jnp.swapaxes(row_ref[...], 0, 1)

    @pl.when(pl.program_id(0) >= tiles)
    def _():
        out_ref[...] = jnp.swapaxes(col_ref[...], 0, 1)


def block_major(row_table, col_table):
    pos, blocks, width = row_table.shape
    tiles = blocks // 8
    return pl.pallas_call(
        block_major_kernel,
        grid=(2 * tiles,),
        in_specs=[
            pl.BlockSpec((pos, 8, width), lambda i: (0, jnp.minimum(i, tiles - 1), 0)),
            pl.BlockSpec((pos, 8, width), lambda i: (0, jnp.maximum(i - tiles, 0), 0)),
        ],
        out_specs=pl.BlockSpec((8, pos, width), lambda i: (i, 0, 0)),
        out_shape=jax.ShapeDtypeStruct((2 * blocks, pos, width), F32),
        compiler_params=params(),
        cost_estimate=COST,
        name="block_major",
    )(row_table, col_table)


def pick_kernel(plans, scalars, sources, *refs):
    scalar_refs = refs[:scalars]
    src_refs = refs[scalars : scalars + sources]
    out_refs = refs[scalars + sources :]
    for out_ref, pieces in zip(out_refs, plans):
        for source, index, table, at_unit, lanes in pieces:
            src_ref, index_ref = src_refs[source], scalar_refs[index]
            table_ref = None if table is None else scalar_refs[table]
            start, stop = lanes
            if at_unit is None:

                def step(j, carry, src_ref=src_ref, index_ref=index_ref, table_ref=table_ref, out_ref=out_ref, start=start, stop=stop):
                    at = index_ref[j]
                    at = at if table_ref is None else table_ref[at]
                    out_ref[j] = src_ref[at, :, start:stop]
                    return carry

                lax.fori_loop(0, out_ref.shape[0], step, 0)
            else:
                named = out_ref.shape[2]

                def step(j, carry, src_ref=src_ref, index_ref=index_ref, table_ref=table_ref, out_ref=out_ref, at_unit=at_unit, named=named):
                    for k in range(named):
                        at = index_ref[j * named + k]
                        at = at if table_ref is None else table_ref[at]
                        out_ref[j, at_unit, k] = src_ref[at]
                    return carry

                lax.fori_loop(0, out_ref.shape[0], step, 0)


def pick(sources, outputs):
    scalars, plans = [], []

    def number(x):
        for at, known in enumerate(scalars):
            if known is x:
                return at
        scalars.append(x)
        return len(scalars) - 1

    for shape, pieces in outputs:
        plan = []
        for source, index, table, unit, lanes in pieces:
            lanes = (0, shape[-1]) if lanes is None else lanes
            plan.append((source, number(index), None if table is None else number(table), unit, lanes))
        plans.append(tuple(plan))
    zeros = lambda shape: lambda i, *_: (0,) * len(shape)
    return pl.pallas_call(
        functools.partial(pick_kernel, tuple(plans), len(scalars), len(sources)),
        grid_spec=pltpu.PrefetchScalarGridSpec(
            num_scalar_prefetch=len(scalars),
            grid=(1,),
            in_specs=[pl.BlockSpec(x.shape, zeros(x.shape)) for x in sources],
            out_specs=[pl.BlockSpec(shape, zeros(shape)) for shape, _ in outputs],
        ),
        out_shape=[jax.ShapeDtypeStruct(shape, F32) for shape, _ in outputs],
        compiler_params=params(),
        cost_estimate=COST,
        name="pick",
    )(*scalars, *sources)


def place_kernel(plans, *refs):
    scalars = refs[: 2 * len(plans)]
    sources = refs[2 * len(plans) : -1]
    out_ref = refs[-1]
    out_ref[...] = jnp.zeros_like(out_ref)
    at_source = 0
    for number, (count, mapped, lanes) in enumerate(plans):
        index_ref, map_ref = scalars[2 * number], scalars[2 * number + 1]
        for start, stop in lanes:
            src_ref = sources[at_source]
            at_source += 1
            named = src_ref.shape[2] if len(src_ref.shape) == 5 else 1

            def step(j, carry, src_ref=src_ref, index_ref=index_ref, map_ref=map_ref, mapped=mapped, start=start, stop=stop, named=named):
                for k in range(named):
                    at = index_ref[j * named + k]
                    at = map_ref[at] if mapped else at
                    block = src_ref[j, 0, k] if len(src_ref.shape) == 5 else src_ref[j]
                    out_ref[at, :, start:stop] += block
                return carry

            lax.fori_loop(0, count // named, step, 0)


def place(terms, count):
    plans, scalars, sources, specs = [], [], [], []
    for arrays, index, table in terms:
        lanes, at = [], 0
        for array, unit in arrays:
            lanes.append((at, at + array.shape[-1]))
            at += array.shape[-1]
            sources.append(array)
            if array.ndim == 5:
                group, _, named, pos, part = array.shape
                entries = group * named
                specs.append(pl.BlockSpec((group, 1, named, pos, part), lambda i, *_, unit=unit: (0, unit, 0, 0, 0)))
            else:
                entries, pos, _ = array.shape
                specs.append(pl.BlockSpec(array.shape, lambda i, *_: (0, 0, 0)))
        plans.append((entries, table is not None, tuple(lanes)))
        scalars += [index, index if table is None else table]
        width = at
    return pl.pallas_call(
        functools.partial(place_kernel, tuple(plans)),
        grid_spec=pltpu.PrefetchScalarGridSpec(
            num_scalar_prefetch=len(scalars),
            grid=(1,),
            in_specs=specs,
            out_specs=pl.BlockSpec((count, pos, width), lambda i, *_: (0, 0, 0)),
        ),
        out_shape=jax.ShapeDtypeStruct((count, pos, width), F32),
        compiler_params=params(),
        cost_estimate=COST,
        name="place",
    )(*scalars, *sources)


def scaled_kernel(pieces, planes, plane_ref, *refs):
    count = len(pieces)
    row_refs, col_refs = refs[:count], refs[count : 2 * count]
    counts_ref, u_ref, v_ref = refs[2 * count : 2 * count + 3]
    s_hi, s_lo, r_hi, r_lo, c_hi, c_lo = refs[2 * count + 3 :]
    step = pl.program_id(1)
    plane = plane_ref[0]
    rows = s_hi.shape[1]
    size = s_hi.shape[2]
    tile = size // planes

    @pl.when(step == 0)
    def _():
        for number, (unit, start, stop) in enumerate(pieces):
            at = pl.multiple_of(lax.bitwise_xor(plane, unit) * tile, tile)
            for src, hi_ref, lo_ref in ((row_refs[number], r_hi, r_lo), (col_refs[number], c_hi, c_lo)):
                hi, lo = split(src[...].reshape(tile, stop - start))
                hi_ref[0, pl.ds(at, tile), start:stop] = hi
                lo_ref[0, pl.ds(at, tile), start:stop] = lo

    mine = pl.ds(pl.multiple_of(step * rows, rows), rows)
    logits = dot3(r_hi[0, mine, :], r_lo[0, mine, :], c_hi[0], c_lo[0], ((1,), (1,)))
    tile_counts = counts_ref[0]
    values = tile_counts.astype(F32)
    target = jnp.log(jnp.maximum(values, 1.0)) - u_ref[0] - v_ref[0]
    error = logits - target
    confidence = 0.1 + 0.25 * jnp.sqrt(values)
    scaled = jnp.where(tile_counts > 0, confidence * error, jax.nn.sigmoid(error)) * (1.0 / size)
    hi, lo = split(scaled)
    s_hi[0] = hi
    s_lo[0] = lo


def scaled_parts(pieces, counts, u, v, plane, planes, first=0, shards=None):
    every, size, _ = counts.shape
    shards = shards or every
    steps = max(planes, 4)
    rows = size // steps
    layout = tuple((unit, first, first + array.shape[4]) for unit, array, _, first in pieces)
    width = max(stop for _, _, stop in layout)
    in_specs = []
    for kind in (0, 1):
        for _, array, at, _ in pieces:
            group, _, _, pos, part = array.shape
            in_specs.append(
                pl.BlockSpec((group, 1, 1, pos, part), lambda s, i, z, kind=kind, at=at: (0, at, 2 * s + kind, 0, 0))
            )
    arrays = [array for _, array, _, _ in pieces]
    in_specs += [
        pl.BlockSpec((1, rows, size), lambda s, i, z: (s + first, i, 0)),
        pl.BlockSpec((1, rows, 1), lambda s, i, z: (s + first, i, 0)),
        pl.BlockSpec((1, 1, size), lambda s, i, z: (s + first, 0, 0)),
    ]
    tile_spec = pl.BlockSpec((1, rows, size), lambda s, i, z: (s, i, 0))
    whole_spec = pl.BlockSpec((1, size, width), lambda s, i, z: (s, 0, 0))
    return pl.pallas_call(
        functools.partial(scaled_kernel, layout, planes),
        grid_spec=pltpu.PrefetchScalarGridSpec(
            num_scalar_prefetch=1,
            grid=(shards, steps),
            in_specs=in_specs,
            out_specs=[tile_spec] * 2 + [whole_spec] * 4,
        ),
        out_shape=[jax.ShapeDtypeStruct((shards, size, size), BF16)] * 2
        + [jax.ShapeDtypeStruct((shards, size, width), BF16)] * 4,
        compiler_params=params(),
        cost_estimate=COST,
        name="scaled",
    )(plane, *arrays, *arrays, counts, u, v)


def grads_kernel(units, plane_ref, *refs):
    tiles, (r_hi, r_lo, c_hi, c_lo, out_ref) = refs[: 4 * units], refs[4 * units :]
    group, _, _, pos, part = out_ref.shape
    for at in range(units):
        sr_hi, sr_lo, sc_hi, sc_lo = tiles[4 * at : 4 * at + 4]
        row_grad = dot3(sr_hi[0], sr_lo[0], c_hi[0], c_lo[0], ((1,), (0,)))
        out_ref[:, at, 0] = row_grad.reshape(group, pos, part)
        col_grad = dot3(sc_hi[0], sc_lo[0], r_hi[0], r_lo[0], ((0,), (0,)))
        out_ref[:, at, 1] = col_grad.reshape(group, pos, part)


def grads(parts, plane, units, chunk, chunks, planes, group, pos):
    s_hi, s_lo, r_hi, r_lo, c_hi, c_lo = parts
    shards, size, width = r_hi.shape
    tile, part = size // planes, width // chunks
    specs = []
    for unit in units:
        rows = pl.BlockSpec((1, tile, size), lambda s, z, unit=unit: (s, lax.bitwise_xor(z[0], unit), 0))
        cols = pl.BlockSpec((1, size, tile), lambda s, z, unit=unit: (s, 0, lax.bitwise_xor(z[0], unit)))
        specs += [rows, rows, cols, cols]
    block = pl.BlockSpec((1, size, part), lambda s, z: (s, 0, chunk))
    return pl.pallas_call(
        functools.partial(grads_kernel, len(units)),
        grid_spec=pltpu.PrefetchScalarGridSpec(
            num_scalar_prefetch=1,
            grid=(shards,),
            in_specs=specs + [block] * 4,
            out_specs=pl.BlockSpec((group, len(units), 2, pos, part), lambda s, z: (0, 0, s, 0, 0)),
        ),
        out_shape=jax.ShapeDtypeStruct((group, len(units), 2 * shards, pos, part), F32),
        compiler_params=params(),
        cost_estimate=COST,
        name="grads",
    )(plane, *([s_hi, s_lo, s_hi, s_lo] * len(units)), r_hi, r_lo, c_hi, c_lo)


def update_kernel(grad_ref, table_ref, accum_ref, new_table_ref, new_accum_ref):
    grad = jnp.swapaxes(grad_ref[...], 0, 1)
    accum = accum_ref[...] + grad * grad
    new_accum_ref[...] = accum
    new_table_ref[...] = table_ref[...] - grad / jnp.sqrt(accum)


def update(grad, table, accum, first):
    pos, blocks, width = table.shape
    spec = pl.BlockSpec((pos, 8, width), lambda i: (0, i, 0))
    return pl.pallas_call(
        update_kernel,
        grid=(blocks // 8,),
        in_specs=[pl.BlockSpec((8, pos, width), lambda i: (i + first // 8, 0, 0)), spec, spec],
        out_specs=[spec, spec],
        out_shape=[jax.ShapeDtypeStruct(table.shape, F32)] * 2,
        compiler_params=params(),
        cost_estimate=COST,
        name="update",
    )(grad, table, accum)


def body(
    row_table, col_table, row_accum, col_accum, row_margin, col_margin, row_blocks, col_blocks, slot_of, counts, *, devices
):
    planes = min(devices // LEAST_GROUP, counts.shape[1] // LANES)
    group = devices // planes
    stages = planes.bit_length() - 1
    shards = row_blocks.shape[0]
    pos, blocks, width = row_table.shape
    size = counts.shape[1]
    slots = 2 * blocks
    named = 2 * shards
    plane = lax.axis_index("dev") // group
    groups = [[group * z + c for c in range(group)] for z in range(planes)]

    def across(x, stage):
        return lax.ppermute(x, "dev", [(d, d ^ (group << stage)) for d in range(devices)])

    def inside(x):
        return lax.all_to_all(x, "dev", 0, 0, axis_index_groups=groups, tiled=True)

    own_ids = jnp.stack([row_blocks, col_blocks], axis=1)
    every = jnp.arange(blocks, dtype=jnp.int32)
    own_slots = jnp.sum(jnp.where(own_ids[:, :, None] == every, slot_of, 0), axis=2)
    own_slots = (own_slots + jnp.array([0, blocks], jnp.int32)).reshape(named).astype(F32)
    margins = jnp.concatenate([row_margin, col_margin], axis=1).reshape(-1)
    told = jnp.concatenate([jnp.pad(own_slots, (0, LANES - named)), margins])
    told = lax.all_to_all(jnp.broadcast_to(told, (devices, told.shape[0])), "dev", 0, 0, tiled=True)
    named_slots = told[:, :named].astype(jnp.int32)

    tables = block_major(row_table, col_table)

    every = jnp.arange(slots, dtype=jnp.int32)
    member = jnp.any(named_slots[:, :, None] == every, axis=1)
    upto = (every[:, None] <= every[None, :]).astype(F32)
    lists, ranks, most = [], [], []
    for stage in range(stages):
        held = jnp.any(member.reshape(planes >> stage, group << stage, slots), axis=1)
        rank = jnp.dot(held.astype(F32), upto, preferred_element_type=F32).astype(jnp.int32) - 1
        most.append(jnp.max(rank[:, -1]) + 1)
        cap = min(slots, named * (group << stage))
        theirs = lax.bitwise_xor(plane, 1 << stage) >> stage
        their_held = lax.dynamic_index_in_dim(held, theirs, 0, keepdims=False)
        their_rank = lax.dynamic_index_in_dim(rank, theirs, 0, keepdims=False)
        hit = (their_rank[None, :] == jnp.arange(cap, dtype=jnp.int32)[:, None]) & their_held[None, :]
        lists.append(jnp.sum(jnp.where(hit, every[None, :], 0), axis=1))
        ours = lax.dynamic_index_in_dim(rank, plane >> stage, 0, keepdims=False)
        ranks.append(jnp.maximum(ours, 0))
    entries = lax.dynamic_slice_in_dim(named_slots, plane * group, group, 0).reshape(group * named)
    plane_arg = plane.reshape(1).astype(jnp.int32)

    def margins_of(told):
        margins = told[:, LANES:].reshape(size, slots)
        mine = lax.dynamic_index_in_dim(named_slots, lax.axis_index("dev"), 0, keepdims=False)
        margins = jnp.sum(jnp.where(mine[:, None, None] == every, margins, 0.0), axis=2).reshape(shards, 2, size)
        return margins[:, 0, :, None], margins[:, 1, None, :]

    def direct(tables, told):
        shape = (group, 1, 2, pos, width)
        u, v = margins_of(told)
        got, index = [], []
        for shard in range(shards):
            index.append(named_slots[:, 2 * shard : 2 * shard + 2].reshape(2 * group))
            after = lax.optimization_barrier((index[-1], *got))[0] if got else index[-1]
            (sent,) = pick([tables], [(shape, [(0, after, None, 0, None)])])
            got.append(inside(sent))
        terms = []
        for shard in range(shards):
            parts = scaled_parts([(0, got[shard], 0, 0)], counts, u, v, plane_arg, planes, shard, 1)
            grad = grads(parts, plane_arg, (0,), 0, 1, planes, group, pos)
            terms.append(([(inside(grad), 0)], index[shard], None))
        grad = place(terms, slots)
        new_row_table, new_row_accum = update(grad, row_table, row_accum, 0)
        new_col_table, new_col_accum = update(grad, col_table, col_accum, blocks)
        return (new_row_table, new_col_table, new_row_accum, new_col_accum)

    if planes == 1:
        return direct(tables, told)

    def step(caps, tables, told):
        def table_of(unit):
            return None if unit == 0 else ranks[lowest_bit(unit)]

        before = []

        def gate(small, *waits):
            return lax.optimization_barrier((small, *before, *waits))[0] if before or waits else small

        def ran(x):
            before[:] = [x]
            return x

        def swap(x, work=lambda: ()):
            if planes != 4:
                return inside(x), work()
            got, done = lax.cond(most[0] > 0, lambda y: (inside(y), work()), lambda y: (y, work()), x)
            return ran(got), done

        source, pieces = {}, []
        def spread(unit, chunk, chunks):
            part = width // chunks
            shape = (group, 1, named, pos, part)
            (sent,) = pick([source[unit, chunk]], [(shape, [(0, gate(entries), table_of(unit), 0, None)])])
            got, _ = swap(ran(sent))
            pieces.append((unit, got, 0, chunk * part))

        source[0, 0] = tables
        chunks = 2 if planes == 4 else 1
        part = width // chunks
        if planes == 4:

            held = []

            def bring(chunk):
                lanes = (chunk * part, (chunk + 1) * part)
                near, far = pick(
                    [tables],
                    [
                        ((caps[0], pos, part), [(0, gate(lists[0]), None, None, lanes)]),
                        ((caps[1], pos, part), [(0, lists[1], None, None, lanes)]),
                    ],
                )
                ran(near)
                held.append((chunk, near, far))

            def leave(*waits):
                for chunk, near, far in held:
                    if waits:
                        near, far, *_ = lax.optimization_barrier((near, far, *waits))
                    source[1, chunk] = across(near, 0)
                    source[2, chunk] = across(far, 1)
                held.clear()

            def relay(chunk):
                (sent,) = pick([source[2, chunk]], [((caps[0], pos, part), [(0, gate(lists[0]), ranks[1], None, None)])])
                source[3, chunk] = across(ran(sent), 0)

            def spread_far(chunk):
                index = gate(entries)
                shape = (group, 2, named, pos, part)
                (sent,) = pick(
                    [source[2, chunk], source[3, chunk]],
                    [(shape, [(0, index, ranks[1], 0, None), (1, index, ranks[0], 1, None)])],
                )
                got, _ = swap(ran(sent))
                pieces.append((2, got, 0, chunk * part))
                pieces.append((3, got, 1, chunk * part))

            bring(0)
            leave()
            bring(1)
            spread(0, 0, 1)
            leave(*before, source[1, 0])
            spread(1, 0, 2)
            relay(0)
            spread(2, 0, 2)
            spread(1, 1, 2)
            relay(1)
            spread(3, 0, 2)
            spread_far(1)
        else:
            for stage in reversed(range(stages)):
                for unit in range(0, planes, 2 << stage):
                    shape = (caps[stage], pos, width)
                    (sent,) = pick([source[unit, 0]], [(shape, [(0, lists[stage], table_of(unit), None, None)])])
                    source[unit ^ (1 << stage), 0] = across(sent, stage)
            for unit in range(planes):
                spread(unit, 0, 1)

        u, v = margins_of(told)
        parts = scaled_parts(pieces, counts, u, v, plane_arg, planes)
        ran(parts[0])

        arrived, passed = {}, {}

        def differentiate(units, chunk, chunks):
            return grads(parts, gate(plane_arg), units, chunk, chunks, planes, group, pos)

        def swap_back(grad, units, chunk, after=None):
            work = (lambda: differentiate(*after)) if after else (lambda: ())
            got, following = swap(grad, work)
            for at, unit in enumerate(units):
                arrived[unit, chunk] = (got, at)
            return following

        def give(unit, chunk, *waits):
            stage = lowest_bit(unit)
            terms = [([arrived[unit, chunk]], gate(entries, *waits), ranks[stage])]
            for lower in range(stage):
                terms.append(([(passed[unit ^ (1 << lower), chunk], 0)], lists[lower], ranks[stage]))
            passed[unit, chunk] = across(ran(place(terms, caps[stage])), stage)

        if planes == 4:
            order = [((3,), 0, 2), ((2,), 0, 2), ((2, 3), 1, 2), ((1,), 0, 2), ((1,), 1, 2), ((0,), 0, 1), None]
            grad = ran(differentiate(*order[0]))
            for at, (units, chunk, _) in enumerate(order[:-1]):
                grad = swap_back(grad, units, chunk, order[at + 1])
                if at == 0:
                    give(3, 0)
                elif at == 1:
                    give(2, 0)
                elif at == 2:
                    give(3, 1)
                elif at == 3:
                    give(2, 1, passed[2, 0])
                    give(1, 0)
                elif at == 4:
                    give(1, 1, passed[1, 0])
        else:
            for unit in reversed(range(planes)):
                swap_back(ran(differentiate((unit,), 0, 1)), (unit,), 0)
            for stage in range(stages):
                for unit in reversed(range(1, planes)):
                    if lowest_bit(unit) == stage:
                        give(unit, 0)
        terms = [([arrived[0, 0]], entries, None)]
        for stage in range(stages):
            arrays = [(passed[1 << stage, chunk], 0) for chunk in range(4) if (1 << stage, chunk) in passed]
            terms.append((arrays, lists[stage], None))
        grad = place(terms, slots)
        new_row_table, new_row_accum = update(grad, row_table, row_accum, 0)
        new_col_table, new_col_accum = update(grad, col_table, col_accum, blocks)
        return (new_row_table, new_col_table, new_row_accum, new_col_accum)

    largest = tuple(min(slots, named * (group << stage)) for stage in range(stages))
    levels = [largest]
    if planes == 4:
        levels = [(largest[0] * k // 64, largest[1] * n // 64) for k, n in ((44, 32), (48, 34), (52, 38))] + levels
    if len(levels) == 1:
        return step(levels[0], tables, told)
    level = jnp.int32(0)
    for caps in levels[:-1]:
        fits = jnp.bool_(True)
        for cap, need in zip(caps, most):
            fits = fits & (need <= cap)
        level = level + jnp.where(fits, 0, 1)
    return lax.switch(level, [functools.partial(step, caps) for caps in levels], tables, told)


def solution(mesh):
    spec = P("dev", None, None)
    flat = P("dev", None)
    return jax.shard_map(
        functools.partial(body, devices=mesh.shape["dev"]),
        mesh=mesh,
        in_specs=(spec, spec, spec, spec, flat, flat, P("dev"), P("dev"), P(), spec),
        out_specs=(spec, spec, spec, spec),
        check_vma=False,
    )
```

```python
import functools

import jax
import jax.numpy as jnp
from jax import lax
from jax.experimental import pallas as pl
from jax.experimental.pallas import tpu as pltpu
from jax.sharding import PartitionSpec as P

LANES = 128
VMEM_LIMIT = 56 * 1024 * 1024
F32 = jnp.float32
BF16 = jnp.bfloat16
COST = pl.CostEstimate(flops=1, bytes_accessed=1, transcendentals=0)


def params():
    return pltpu.CompilerParams(vmem_limit_bytes=VMEM_LIMIT)


def split(x):
    hi = x.astype(BF16)
    return hi, (x - hi.astype(F32)).astype(BF16)


def dot3(a_hi, a_lo, b_hi, b_lo, dims):
    def dot(a, b):
        return lax.dot_general(a, b, (dims, ((), ())), preferred_element_type=F32)

    return dot(a_hi, b_hi) + dot(a_hi, b_lo) + dot(a_lo, b_hi)


def block_major_kernel(row_ref, col_ref, out_ref):
    tiles = pl.num_programs(0) // 2

    @pl.when(pl.program_id(0) < tiles)
    def _():
        out_ref[...] = jnp.swapaxes(row_ref[...], 0, 1)

    @pl.when(pl.program_id(0) >= tiles)
    def _():
        out_ref[...] = jnp.swapaxes(col_ref[...], 0, 1)


def block_major(row_table, col_table):
    pos, blocks, width = row_table.shape
    tiles = blocks // 8
    return pl.pallas_call(
        block_major_kernel,
        grid=(2 * tiles,),
        in_specs=[
            pl.BlockSpec((pos, 8, width), lambda i: (0, jnp.minimum(i, tiles - 1), 0)),
            pl.BlockSpec((pos, 8, width), lambda i: (0, jnp.maximum(i - tiles, 0), 0)),
        ],
        out_specs=pl.BlockSpec((8, pos, width), lambda i: (i, 0, 0)),
        out_shape=jax.ShapeDtypeStruct((2 * blocks, pos, width), F32),
        compiler_params=params(),
        cost_estimate=COST,
        name="block_major",
    )(row_table, col_table)


def pick_kernel(index_ref, src_ref, out_ref):
    def step(j, carry):
        for k in range(out_ref.shape[1]):
            out_ref[j, k] = src_ref[index_ref[j * out_ref.shape[1] + k]]
        return carry

    lax.fori_loop(0, out_ref.shape[0], step, 0)


def pick(blocks, index, count):
    entries = index.shape[0]
    shape = (entries // count, count) + blocks.shape[1:]
    return pl.pallas_call(
        pick_kernel,
        grid_spec=pltpu.PrefetchScalarGridSpec(
            num_scalar_prefetch=1,
            grid=(1,),
            in_specs=[pl.BlockSpec(blocks.shape, lambda i, *_: (0, 0, 0))],
            out_specs=pl.BlockSpec(shape, lambda i, *_: (0, 0, 0, 0)),
        ),
        out_shape=jax.ShapeDtypeStruct(shape, F32),
        compiler_params=params(),
        cost_estimate=COST,
        name="pick",
    )(index, blocks)


def scaled_kernel(got_row, got_col, counts_ref, u_ref, v_ref, s_hi, s_lo, r_hi, r_lo, c_hi, c_lo):
    step = pl.program_id(0)
    rows, size = s_hi.shape

    @pl.when(step == 0)
    def _():
        for src, hi_ref, lo_ref in ((got_row, r_hi, r_lo), (got_col, c_hi, c_lo)):
            hi, lo = split(src[...].reshape(hi_ref.shape))
            hi_ref[...] = hi
            lo_ref[...] = lo

    mine = pl.ds(pl.multiple_of(step * rows, rows), rows)
    logits = dot3(r_hi[mine, :], r_lo[mine, :], c_hi[...], c_lo[...], ((1,), (1,)))
    tile_counts = counts_ref[0]
    values = tile_counts.astype(F32)
    target = jnp.log(jnp.maximum(values, 1.0)) - u_ref[0] - v_ref[0]
    error = logits - target
    confidence = 0.1 + 0.25 * jnp.sqrt(values)
    scaled = jnp.where(tile_counts > 0, confidence * error, jax.nn.sigmoid(error)) * (1.0 / size)
    hi, lo = split(scaled)
    s_hi[...] = hi
    s_lo[...] = lo


def scaled_parts(got, counts, u, v, shard, steps):
    size = counts.shape[1]
    devices, _, pos, width = got.shape
    rows = size // steps
    tile = pl.BlockSpec((rows, size), lambda i: (i, 0))
    whole = pl.BlockSpec((size, width), lambda i: (0, 0))
    return pl.pallas_call(
        scaled_kernel,
        grid=(steps,),
        in_specs=[
            pl.BlockSpec((devices, 1, pos, width), lambda i: (0, 0, 0, 0)),
            pl.BlockSpec((devices, 1, pos, width), lambda i: (0, 1, 0, 0)),
            pl.BlockSpec((1, rows, size), lambda i: (shard, i, 0)),
            pl.BlockSpec((1, rows, 1), lambda i: (shard, i, 0)),
            pl.BlockSpec((1, 1, size), lambda i: (shard, 0, 0)),
        ],
        out_specs=[tile] * 2 + [whole] * 4,
        out_shape=[jax.ShapeDtypeStruct((size, size), BF16)] * 2 + [jax.ShapeDtypeStruct((size, width), BF16)] * 4,
        compiler_params=params(),
        cost_estimate=COST,
        name="scaled",
    )(got, got, counts, u, v)


def grads_kernel(sr_hi, sr_lo, sc_hi, sc_lo, r_hi, r_lo, c_hi, c_lo, out_ref):
    devices, _, pos, width = out_ref.shape
    row_grad = dot3(sr_hi[...], sr_lo[...], c_hi[...], c_lo[...], ((1,), (0,)))
    out_ref[:, 0] = row_grad.reshape(devices, pos, width)
    col_grad = dot3(sc_hi[...], sc_lo[...], r_hi[...], r_lo[...], ((0,), (0,)))
    out_ref[:, 1] = col_grad.reshape(devices, pos, width)


def grads(parts, pos, steps):
    s_hi, s_lo, r_hi, r_lo, c_hi, c_lo = parts
    size, width = r_hi.shape
    rows = size // steps
    held = rows // pos
    across = pl.BlockSpec((rows, size), lambda i: (i, 0))
    down = pl.BlockSpec((size, rows), lambda i: (0, i))
    whole = pl.BlockSpec((size, width), lambda i: (0, 0))
    return pl.pallas_call(
        grads_kernel,
        grid=(steps,),
        in_specs=[across, across, down, down] + [whole] * 4,
        out_specs=pl.BlockSpec((held, 2, pos, width), lambda i: (i, 0, 0, 0)),
        out_shape=jax.ShapeDtypeStruct((size // pos, 2, pos, width), F32),
        compiler_params=params(),
        cost_estimate=COST,
        name="grads",
    )(s_hi, s_lo, s_hi, s_lo, r_hi, r_lo, c_hi, c_lo)


def update_kernel(sources, *refs):
    index_refs, refs = refs[:sources], refs[sources:]
    source_refs = refs[:sources]
    row, row_acc, col, col_acc, new_row, new_col, new_row_acc, new_col_acc, grad_ref = refs[sources:]
    step, tiles = pl.program_id(0), pl.num_programs(0) // 2

    @pl.when(step == 0)
    def _():
        grad_ref[...] = jnp.zeros_like(grad_ref)
        for index_ref, source_ref in zip(index_refs, source_refs):
            count = source_ref.shape[1]

            def add(j, carry, index_ref=index_ref, source_ref=source_ref, count=count):
                for k in range(count):
                    grad_ref[index_ref[j * count + k]] += source_ref[j, k]
                return carry

            lax.fori_loop(0, source_ref.shape[0], add, 0)

    def move(table_ref, accum_ref, new_table_ref, new_accum_ref):
        grad = jnp.swapaxes(grad_ref[pl.ds(pl.multiple_of(step * 8, 8), 8)], 0, 1)
        accum = accum_ref[...] + grad * grad
        new_accum_ref[...] = accum
        new_table_ref[...] = table_ref[...] - grad / jnp.sqrt(accum)

    @pl.when(step < tiles)
    def _():
        move(row, row_acc, new_row, new_row_acc)

    @pl.when(step >= tiles)
    def _():
        move(col, col_acc, new_col, new_col_acc)


def update(indices, sources, row_table, col_table, row_accum, col_accum):
    pos, blocks, width = row_table.shape
    tiles = blocks // 8
    row = pl.BlockSpec((pos, 8, width), lambda i, *_: (0, jnp.minimum(i, tiles - 1), 0))
    col = pl.BlockSpec((pos, 8, width), lambda i, *_: (0, jnp.maximum(i - tiles, 0), 0))
    return pl.pallas_call(
        functools.partial(update_kernel, len(sources)),
        grid_spec=pltpu.PrefetchScalarGridSpec(
            num_scalar_prefetch=len(indices),
            grid=(2 * tiles,),
            in_specs=[pl.BlockSpec(x.shape, lambda i, *_: (0, 0, 0, 0)) for x in sources] + [row, row, col, col],
            out_specs=[row, col, row, col],
            scratch_shapes=[pltpu.VMEM((2 * blocks, pos, width), F32)],
        ),
        out_shape=[jax.ShapeDtypeStruct(row_table.shape, F32)] * 4,
        compiler_params=params(),
        cost_estimate=COST,
        name="update",
    )(*indices, *sources, row_table, row_accum, col_table, col_accum)


def body(
    row_table, col_table, row_accum, col_accum, row_margin, col_margin, row_blocks, col_blocks, slot_of, counts, *, devices
):
    shards, size, _ = counts.shape
    pos, blocks, width = row_table.shape
    slots = 2 * blocks
    steps = 4

    def swap(x):
        return lax.all_to_all(x, "dev", 0, 0, tiled=True)

    every = jnp.arange(blocks, dtype=jnp.int32)
    ids = jnp.stack([row_blocks, col_blocks], axis=1)
    named = jnp.sum(jnp.where(ids[:, :, None] == every, slot_of, 0), axis=2) + jnp.array([0, blocks], jnp.int32)
    margins = jnp.concatenate([row_margin, col_margin], axis=1).reshape(-1)
    told = jnp.concatenate([jnp.pad(named.reshape(-1).astype(F32), (0, LANES - 2 * shards)), margins])
    told = swap(jnp.broadcast_to(told, (devices, told.shape[0])))
    tables = block_major(row_table, col_table)
    index = [told[:, 2 * shard : 2 * shard + 2].astype(jnp.int32).reshape(-1) for shard in range(shards)]

    sent, got = [], []
    for shard in range(shards):
        after = lax.optimization_barrier((index[shard], sent[-1]))[0] if sent else index[shard]
        sent.append(pick(tables, after, 2))
        got.append(swap(sent[-1]))

    margins = told[:, LANES:].reshape(size, slots)
    mine = named.reshape(2 * shards)
    margins = jnp.sum(jnp.where(mine[:, None, None] == jnp.arange(slots, dtype=jnp.int32), margins, 0.0), axis=2)
    margins = margins.reshape(shards, 2, size)
    u, v = margins[:, 0, :, None], margins[:, 1, None, :]

    back = []
    for shard in range(shards):
        parts = scaled_parts(got[shard], counts, u, v, shard, steps)
        back.append(swap(grads(parts, pos, steps)))
    return tuple(update(index, back, row_table, col_table, row_accum, col_accum))


def solution(mesh):
    spec = P("dev", None, None)
    flat = P("dev", None)
    return jax.shard_map(
        functools.partial(body, devices=mesh.shape["dev"]),
        mesh=mesh,
        in_specs=(spec, spec, spec, spec, flat, flat, P("dev"), P("dev"), P(), spec),
        out_specs=(spec, spec, spec, spec),
        check_vma=False,
    )
```

```python
import functools

import jax
import jax.numpy as jnp
from jax import lax
from jax.experimental import pallas as pl
from jax.experimental.pallas import tpu as pltpu
from jax.sharding import PartitionSpec as P

LANES = 128
VMEM_LIMIT = 56 * 1024 * 1024
F32 = jnp.float32
BF16 = jnp.bfloat16
COST = pl.CostEstimate(flops=1, bytes_accessed=1, transcendentals=0)


def params():
    return pltpu.CompilerParams(vmem_limit_bytes=VMEM_LIMIT)


def split(x):
    hi = x.astype(BF16)
    return hi, (x - hi.astype(F32)).astype(BF16)


def dot3(a_hi, a_lo, b_hi, b_lo, dims):
    def dot(a, b):
        return lax.dot_general(a, b, (dims, ((), ())), preferred_element_type=F32)

    return dot(a_hi, b_hi) + dot(a_hi, b_lo) + dot(a_lo, b_hi)


def block_major_kernel(row_ref, col_ref, out_ref):
    tiles = pl.num_programs(0) // 2

    @pl.when(pl.program_id(0) < tiles)
    def _():
        out_ref[...] = jnp.swapaxes(row_ref[...], 0, 1)

    @pl.when(pl.program_id(0) >= tiles)
    def _():
        out_ref[...] = jnp.swapaxes(col_ref[...], 0, 1)


def block_major(row_table, col_table):
    pos, blocks, width = row_table.shape
    tiles = blocks // 8
    return pl.pallas_call(
        block_major_kernel,
        grid=(2 * tiles,),
        in_specs=[
            pl.BlockSpec((pos, 8, width), lambda i: (0, jnp.minimum(i, tiles - 1), 0)),
            pl.BlockSpec((pos, 8, width), lambda i: (0, jnp.maximum(i - tiles, 0), 0)),
        ],
        out_specs=pl.BlockSpec((8, pos, width), lambda i: (i, 0, 0)),
        out_shape=jax.ShapeDtypeStruct((2 * blocks, pos, width), F32),
        compiler_params=params(),
        cost_estimate=COST,
        name="block_major",
    )(row_table, col_table)


def pick_kernel(shard, named_ref, src_ref, out_ref):
    def step(j, carry):
        for k in range(2):
            out_ref[j, k] = src_ref[named_ref[j, 2 * shard + k]]
        return carry

    lax.fori_loop(0, out_ref.shape[0], step, 0)


def pick(blocks, named, shard):
    shape = (named.shape[0], 2) + blocks.shape[1:]
    return pl.pallas_call(
        functools.partial(pick_kernel, shard),
        grid_spec=pltpu.PrefetchScalarGridSpec(
            num_scalar_prefetch=1,
            grid=(1,),
            in_specs=[pl.BlockSpec(blocks.shape, lambda i, *_: (0, 0, 0))],
            out_specs=pl.BlockSpec(shape, lambda i, *_: (0, 0, 0, 0)),
        ),
        out_shape=jax.ShapeDtypeStruct(shape, F32),
        compiler_params=params(),
        cost_estimate=COST,
        name="pick",
    )(named, blocks)


def scaled_kernel(got_row, got_col, counts_ref, u_ref, v_ref, s_hi, s_lo, r_hi, r_lo, c_hi, c_lo):
    step = pl.program_id(0)
    rows, size = s_hi.shape

    @pl.when(step == 0)
    def _():
        for src, hi_ref, lo_ref in ((got_row, r_hi, r_lo), (got_col, c_hi, c_lo)):
            hi, lo = split(src[...].reshape(hi_ref.shape))
            hi_ref[...] = hi
            lo_ref[...] = lo

    mine = pl.ds(pl.multiple_of(step * rows, rows), rows)
    logits = dot3(r_hi[mine, :], r_lo[mine, :], c_hi[...], c_lo[...], ((1,), (1,)))
    tile_counts = counts_ref[0]
    values = tile_counts.astype(F32)
    target = jnp.log(jnp.maximum(values, 1.0)) - u_ref[0] - v_ref[0]
    error = logits - target
    confidence = 0.1 + 0.25 * jnp.sqrt(values)
    scaled = jnp.where(tile_counts > 0, confidence * error, jax.nn.sigmoid(error)) * (1.0 / size)
    hi, lo = split(scaled)
    s_hi[...] = hi
    s_lo[...] = lo


def scaled_parts(got, counts, u, v, shard, steps):
    size = counts.shape[1]
    devices, _, pos, width = got.shape
    rows = size // steps
    tile = pl.BlockSpec((rows, size), lambda i: (i, 0))
    whole = pl.BlockSpec((size, width), lambda i: (0, 0))
    return pl.pallas_call(
        scaled_kernel,
        grid=(steps,),
        in_specs=[
            pl.BlockSpec((devices, 1, pos, width), lambda i: (0, 0, 0, 0)),
            pl.BlockSpec((devices, 1, pos, width), lambda i: (0, 1, 0, 0)),
            pl.BlockSpec((1, rows, size), lambda i: (shard, i, 0)),
            pl.BlockSpec((1, rows, 1), lambda i: (shard, i, 0)),
            pl.BlockSpec((1, 1, size), lambda i: (shard, 0, 0)),
        ],
        out_specs=[tile] * 2 + [whole] * 4,
        out_shape=[jax.ShapeDtypeStruct((size, size), BF16)] * 2 + [jax.ShapeDtypeStruct((size, width), BF16)] * 4,
        compiler_params=params(),
        cost_estimate=COST,
        name="scaled",
    )(got, got, counts, u, v)


def grads_kernel(sr_hi, sr_lo, sc_hi, sc_lo, r_hi, r_lo, c_hi, c_lo, out_ref):
    devices, _, pos, width = out_ref.shape
    row_grad = dot3(sr_hi[...], sr_lo[...], c_hi[...], c_lo[...], ((1,), (0,)))
    out_ref[:, 0] = row_grad.reshape(devices, pos, width)
    col_grad = dot3(sc_hi[...], sc_lo[...], r_hi[...], r_lo[...], ((0,), (0,)))
    out_ref[:, 1] = col_grad.reshape(devices, pos, width)


def grads(parts, pos, steps):
    s_hi, s_lo, r_hi, r_lo, c_hi, c_lo = parts
    size, width = r_hi.shape
    rows = size // steps
    held = rows // pos
    across = pl.BlockSpec((rows, size), lambda i: (i, 0))
    down = pl.BlockSpec((size, rows), lambda i: (0, i))
    whole = pl.BlockSpec((size, width), lambda i: (0, 0))
    return pl.pallas_call(
        grads_kernel,
        grid=(steps,),
        in_specs=[across, across, down, down] + [whole] * 4,
        out_specs=pl.BlockSpec((held, 2, pos, width), lambda i: (i, 0, 0, 0)),
        out_shape=jax.ShapeDtypeStruct((size // pos, 2, pos, width), F32),
        compiler_params=params(),
        cost_estimate=COST,
        name="grads",
    )(s_hi, s_lo, s_hi, s_lo, r_hi, r_lo, c_hi, c_lo)


def add_blocks(shard, named_ref, src_ref, grad_ref):
    def add(j, carry):
        for k in range(2):
            grad_ref[named_ref[j, 2 * shard + k]] += src_ref[j, k]
        return carry

    grad_ref[...] = jnp.zeros_like(grad_ref)
    lax.fori_loop(0, src_ref.shape[0], add, 0)


def place(named, source, shard, slots):
    shape = (slots,) + source.shape[2:]
    return pl.pallas_call(
        functools.partial(add_blocks, shard),
        grid_spec=pltpu.PrefetchScalarGridSpec(
            num_scalar_prefetch=1,
            grid=(1,),
            in_specs=[pl.BlockSpec(source.shape, lambda i, *_: (0, 0, 0, 0))],
            out_specs=pl.BlockSpec(shape, lambda i, *_: (0, 0, 0)),
        ),
        out_shape=jax.ShapeDtypeStruct(shape, F32),
        compiler_params=params(),
        cost_estimate=COST,
        name="place",
    )(named, source)


def update_kernel(shard, placed, named_ref, source_ref, *refs):
    placed_refs, refs = refs[:placed], refs[placed:]
    row, row_acc, col, col_acc, new_row, new_col, new_row_acc, new_col_acc, grad_ref = refs
    step, tiles = pl.program_id(0), pl.num_programs(0) // 2

    @pl.when(step == 0)
    def _():
        add_blocks(shard, named_ref, source_ref, grad_ref)

    def move(table_ref, accum_ref, new_table_ref, new_accum_ref):
        grad = grad_ref[pl.ds(pl.multiple_of(step * 8, 8), 8)]
        for placed_ref in placed_refs:
            grad = grad + placed_ref[...]
        grad = jnp.swapaxes(grad, 0, 1)
        accum = accum_ref[...] + grad * grad
        new_accum_ref[...] = accum
        new_table_ref[...] = table_ref[...] - grad * lax.rsqrt(accum)

    @pl.when(step < tiles)
    def _():
        move(row, row_acc, new_row, new_row_acc)

    @pl.when(step >= tiles)
    def _():
        move(col, col_acc, new_col, new_col_acc)


def update(named, source, shard, placed, row_table, col_table, row_accum, col_accum):
    pos, blocks, width = row_table.shape
    tiles = blocks // 8
    row = pl.BlockSpec((pos, 8, width), lambda i, *_: (0, jnp.minimum(i, tiles - 1), 0))
    col = pl.BlockSpec((pos, 8, width), lambda i, *_: (0, jnp.maximum(i - tiles, 0), 0))
    return pl.pallas_call(
        functools.partial(update_kernel, shard, len(placed)),
        grid_spec=pltpu.PrefetchScalarGridSpec(
            num_scalar_prefetch=1,
            grid=(2 * tiles,),
            in_specs=[pl.BlockSpec(source.shape, lambda i, *_: (0, 0, 0, 0))]
            + [pl.BlockSpec((8, pos, width), lambda i, *_: (i, 0, 0))] * len(placed)
            + [row, row, col, col],
            out_specs=[row, col, row, col],
            scratch_shapes=[pltpu.VMEM((2 * blocks, pos, width), F32)],
        ),
        out_shape=[jax.ShapeDtypeStruct(row_table.shape, F32)] * 4,
        compiler_params=params(),
        cost_estimate=COST,
        name="update",
    )(named, source, *placed, row_table, row_accum, col_table, col_accum)


def body(
    row_table, col_table, row_accum, col_accum, row_margin, col_margin, row_blocks, col_blocks, slot_of, counts, *, devices
):
    shards, size, _ = counts.shape
    pos, blocks, width = row_table.shape
    slots = 2 * blocks
    steps = 4

    def swap(x):
        return lax.all_to_all(x, "dev", 0, 0, tiled=True)

    every = jnp.arange(blocks, dtype=jnp.int32)
    ids = jnp.stack([row_blocks, col_blocks], axis=1)
    mine = jnp.sum(jnp.where(ids[:, :, None] == every, slot_of, 0), axis=2) + jnp.array([0, blocks], jnp.int32)
    mine = mine.reshape(2 * shards)
    margins = jnp.concatenate([row_margin, col_margin], axis=1).reshape(-1)
    told = jnp.concatenate([jnp.pad(mine.astype(F32), (0, LANES - 2 * shards)), margins])
    told = swap(jnp.broadcast_to(told, (devices, told.shape[0])))
    tables = block_major(row_table, col_table)
    named = told[:, :LANES].astype(jnp.int32)

    sent, got = [], []
    for shard in range(shards):
        after = lax.optimization_barrier((named, sent[-1]))[0] if sent else named
        sent.append(pick(tables, after, shard))
        got.append(swap(sent[-1]))

    margins = told[:, LANES:].reshape(size, slots)
    margins = jnp.sum(jnp.where(mine[:, None, None] == jnp.arange(slots, dtype=jnp.int32), margins, 0.0), axis=2)
    margins = margins.reshape(shards, 2, size)
    u, v = margins[:, 0, :, None], margins[:, 1, None, :]

    back = []
    for shard in range(shards):
        parts = scaled_parts(got[shard], counts, u, v, shard, steps)
        back.append(swap(grads(parts, pos, steps)))
    placed = [place(named, back[shard], shard, slots) for shard in range(shards - 1)]
    return tuple(update(named, back[-1], shards - 1, placed, row_table, col_table, row_accum, col_accum))


def solution(mesh):
    spec = P("dev", None, None)
    flat = P("dev", None)
    return jax.shard_map(
        functools.partial(body, devices=mesh.shape["dev"]),
        mesh=mesh,
        in_specs=(spec, spec, spec, spec, flat, flat, P("dev"), P("dev"), P(), spec),
        out_specs=(spec, spec, spec, spec),
        check_vma=False,
    )
```

```python
import functools

import jax
import jax.numpy as jnp
from jax import lax
from jax.experimental import pallas as pl
from jax.experimental.pallas import tpu as pltpu
from jax.sharding import PartitionSpec as P

LANES = 128
VMEM_LIMIT = 56 * 1024 * 1024
F32 = jnp.float32
BF16 = jnp.bfloat16
COST = pl.CostEstimate(flops=1, bytes_accessed=1, transcendentals=0)


def params():
    return pltpu.CompilerParams(vmem_limit_bytes=VMEM_LIMIT)


def split(x):
    hi = x.astype(BF16)
    return hi, (x - hi.astype(F32)).astype(BF16)


def dot3(a_hi, a_lo, b_hi, b_lo, dims):
    def dot(a, b):
        return lax.dot_general(a, b, (dims, ((), ())), preferred_element_type=F32)

    return dot(a_hi, b_hi) + dot(a_hi, b_lo) + dot(a_lo, b_hi)


def block_major_kernel(row_ref, col_ref, out_ref):
    tiles = pl.num_programs(0) // 2

    @pl.when(pl.program_id(0) < tiles)
    def _():
        out_ref[...] = jnp.swapaxes(row_ref[...], 0, 1)

    @pl.when(pl.program_id(0) >= tiles)
    def _():
        out_ref[...] = jnp.swapaxes(col_ref[...], 0, 1)


def block_major(row_table, col_table):
    pos, blocks, width = row_table.shape
    tiles = blocks // 8
    return pl.pallas_call(
        block_major_kernel,
        grid=(2 * tiles,),
        in_specs=[
            pl.BlockSpec((pos, 8, width), lambda i: (0, jnp.minimum(i, tiles - 1), 0)),
            pl.BlockSpec((pos, 8, width), lambda i: (0, jnp.maximum(i - tiles, 0), 0)),
        ],
        out_specs=pl.BlockSpec((8, pos, width), lambda i: (i, 0, 0)),
        out_shape=jax.ShapeDtypeStruct((2 * blocks, pos, width), F32),
        compiler_params=params(),
        cost_estimate=COST,
        name="block_major",
    )(row_table, col_table)


def pick_kernel(shard, named_ref, src_ref, out_ref):
    kind = pl.program_id(0)
    first = kind * src_ref.shape[0]

    def step(j, carry):
        out_ref[j, 0] = src_ref[named_ref[j, 2 * shard + kind] - first]
        return carry

    lax.fori_loop(0, out_ref.shape[0], step, 0)


def pick(blocks, named, shard):
    slots, pos, width = blocks.shape
    devices = named.shape[0]
    return pl.pallas_call(
        functools.partial(pick_kernel, shard),
        grid_spec=pltpu.PrefetchScalarGridSpec(
            num_scalar_prefetch=1,
            grid=(2,),
            in_specs=[pl.BlockSpec((slots // 2, pos, width), lambda i, *_: (i, 0, 0))],
            out_specs=pl.BlockSpec((devices, 1, pos, width), lambda i, *_: (0, i, 0, 0)),
        ),
        out_shape=jax.ShapeDtypeStruct((devices, 2, pos, width), F32),
        compiler_params=params(),
        cost_estimate=COST,
        name="pick",
    )(named, blocks)


def scaled_kernel(got_row, got_col, counts_ref, u_ref, v_ref, s_hi, s_lo, r_hi, r_lo, c_hi, c_lo):
    step = pl.program_id(0)
    rows, size = s_hi.shape

    @pl.when(step == 0)
    def _():
        for src, hi_ref, lo_ref in ((got_row, r_hi, r_lo), (got_col, c_hi, c_lo)):
            hi, lo = split(src[...].reshape(hi_ref.shape))
            hi_ref[...] = hi
            lo_ref[...] = lo

    mine = pl.ds(pl.multiple_of(step * rows, rows), rows)
    logits = dot3(r_hi[mine, :], r_lo[mine, :], c_hi[...], c_lo[...], ((1,), (1,)))
    tile_counts = counts_ref[0]
    values = tile_counts.astype(F32)
    target = jnp.log(jnp.maximum(values, 1.0)) - u_ref[0] - v_ref[0]
    error = logits - target
    confidence = 0.1 + 0.25 * jnp.sqrt(values)
    scaled = jnp.where(tile_counts > 0, confidence * error, jax.nn.sigmoid(error)) * (1.0 / size)
    hi, lo = split(scaled)
    s_hi[...] = hi
    s_lo[...] = lo


def scaled_parts(got, counts, u, v, shard, steps):
    size = counts.shape[1]
    devices, _, pos, width = got.shape
    rows = size // steps
    tile = pl.BlockSpec((rows, size), lambda i: (i, 0))
    whole = pl.BlockSpec((size, width), lambda i: (0, 0))
    return pl.pallas_call(
        scaled_kernel,
        grid=(steps,),
        in_specs=[
            pl.BlockSpec((devices, 1, pos, width), lambda i: (0, 0, 0, 0)),
            pl.BlockSpec((devices, 1, pos, width), lambda i: (0, 1, 0, 0)),
            pl.BlockSpec((1, rows, size), lambda i: (shard, i, 0)),
            pl.BlockSpec((1, rows, 1), lambda i: (shard, i, 0)),
            pl.BlockSpec((1, 1, size), lambda i: (shard, 0, 0)),
        ],
        out_specs=[tile] * 2 + [whole] * 4,
        out_shape=[jax.ShapeDtypeStruct((size, size), BF16)] * 2 + [jax.ShapeDtypeStruct((size, width), BF16)] * 4,
        compiler_params=params(),
        cost_estimate=COST,
        name="scaled",
    )(got, got, counts, u, v)


def grads_kernel(sr_hi, sr_lo, sc_hi, sc_lo, r_hi, r_lo, c_hi, c_lo, out_ref):
    devices, _, pos, width = out_ref.shape
    row_grad = dot3(sr_hi[...], sr_lo[...], c_hi[...], c_lo[...], ((1,), (0,)))
    out_ref[:, 0] = row_grad.reshape(devices, pos, width)
    col_grad = dot3(sc_hi[...], sc_lo[...], r_hi[...], r_lo[...], ((0,), (0,)))
    out_ref[:, 1] = col_grad.reshape(devices, pos, width)


def grads(parts, pos, steps):
    s_hi, s_lo, r_hi, r_lo, c_hi, c_lo = parts
    size, width = r_hi.shape
    rows = size // steps
    held = rows // pos
    across = pl.BlockSpec((rows, size), lambda i: (i, 0))
    down = pl.BlockSpec((size, rows), lambda i: (0, i))
    whole = pl.BlockSpec((size, width), lambda i: (0, 0))
    return pl.pallas_call(
        grads_kernel,
        grid=(steps,),
        in_specs=[across, across, down, down] + [whole] * 4,
        out_specs=pl.BlockSpec((held, 2, pos, width), lambda i: (i, 0, 0, 0)),
        out_shape=jax.ShapeDtypeStruct((size // pos, 2, pos, width), F32),
        compiler_params=params(),
        cost_estimate=COST,
        name="grads",
    )(s_hi, s_lo, s_hi, s_lo, r_hi, r_lo, c_hi, c_lo)


def add_blocks(shard, named_ref, src_ref, grad_ref):
    def add(j, carry):
        for k in range(2):
            grad_ref[named_ref[j, 2 * shard + k]] += src_ref[j, k]
        return carry

    grad_ref[...] = jnp.zeros_like(grad_ref)
    lax.fori_loop(0, src_ref.shape[0], add, 0)


def place(named, source, shard, slots):
    shape = (slots,) + source.shape[2:]
    return pl.pallas_call(
        functools.partial(add_blocks, shard),
        grid_spec=pltpu.PrefetchScalarGridSpec(
            num_scalar_prefetch=1,
            grid=(1,),
            in_specs=[pl.BlockSpec(source.shape, lambda i, *_: (0, 0, 0, 0))],
            out_specs=pl.BlockSpec(shape, lambda i, *_: (0, 0, 0)),
        ),
        out_shape=jax.ShapeDtypeStruct(shape, F32),
        compiler_params=params(),
        cost_estimate=COST,
        name="place",
    )(named, source)


def update_kernel(shard, placed, named_ref, source_ref, *refs):
    placed_refs, refs = refs[:placed], refs[placed:]
    row, row_acc, col, col_acc, new_row, new_col, new_row_acc, new_col_acc, grad_ref = refs
    step, tiles = pl.program_id(0), pl.num_programs(0) // 2

    kind = step // tiles
    inner = step - kind * tiles

    @pl.when(inner == 0)
    def _():
        first = kind * grad_ref.shape[0]

        def add(j, carry):
            grad_ref[named_ref[j, 2 * shard + kind] - first] += source_ref[j, 0]
            return carry

        grad_ref[...] = jnp.zeros_like(grad_ref)
        lax.fori_loop(0, source_ref.shape[0], add, 0)

    def move(table_ref, accum_ref, new_table_ref, new_accum_ref):
        grad = grad_ref[pl.ds(pl.multiple_of(inner * 8, 8), 8)]
        for placed_ref in placed_refs:
            grad = grad + placed_ref[...]
        grad = jnp.swapaxes(grad, 0, 1)
        accum = accum_ref[...] + grad * grad
        new_accum_ref[...] = accum
        new_table_ref[...] = table_ref[...] - grad * lax.rsqrt(accum)

    @pl.when(step < tiles)
    def _():
        move(row, row_acc, new_row, new_row_acc)

    @pl.when(step >= tiles)
    def _():
        move(col, col_acc, new_col, new_col_acc)


def update(named, source, shard, placed, row_table, col_table, row_accum, col_accum):
    pos, blocks, width = row_table.shape
    tiles = blocks // 8
    row = pl.BlockSpec((pos, 8, width), lambda i, *_: (0, jnp.minimum(i, tiles - 1), 0))
    col = pl.BlockSpec((pos, 8, width), lambda i, *_: (0, jnp.maximum(i - tiles, 0), 0))
    return pl.pallas_call(
        functools.partial(update_kernel, shard, len(placed)),
        grid_spec=pltpu.PrefetchScalarGridSpec(
            num_scalar_prefetch=1,
            grid=(2 * tiles,),
            in_specs=[pl.BlockSpec((source.shape[0], 1, pos, width), lambda i, *_: (0, i // tiles, 0, 0))]
            + [pl.BlockSpec((8, pos, width), lambda i, *_: (i, 0, 0))] * len(placed)
            + [row, row, col, col],
            out_specs=[row, col, row, col],
            scratch_shapes=[pltpu.VMEM((blocks, pos, width), F32)],
        ),
        out_shape=[jax.ShapeDtypeStruct(row_table.shape, F32)] * 4,
        compiler_params=params(),
        cost_estimate=COST,
        name="update",
    )(named, source, *placed, row_table, row_accum, col_table, col_accum)


def body(
    row_table, col_table, row_accum, col_accum, row_margin, col_margin, row_blocks, col_blocks, slot_of, counts, *, devices
):
    shards, size, _ = counts.shape
    pos, blocks, width = row_table.shape
    slots = 2 * blocks
    steps = 4

    def swap(x):
        return lax.all_to_all(x, "dev", 0, 0, tiled=True)

    every = jnp.arange(blocks, dtype=jnp.int32)
    ids = jnp.stack([row_blocks, col_blocks], axis=1)
    mine = jnp.sum(jnp.where(ids[:, :, None] == every, slot_of, 0), axis=2) + jnp.array([0, blocks], jnp.int32)
    mine = mine.reshape(2 * shards)
    margins = jnp.concatenate([row_margin, col_margin], axis=1).reshape(-1)
    told = jnp.concatenate([jnp.pad(mine.astype(F32), (0, LANES - 2 * shards)), margins])
    told = swap(jnp.broadcast_to(told, (devices, told.shape[0])))
    tables = block_major(row_table, col_table)
    named = told[:, :LANES].astype(jnp.int32)

    sent, got = [], []
    for shard in range(shards):
        after = lax.optimization_barrier((named, sent[-1]))[0] if sent else named
        sent.append(pick(tables, after, shard))
        got.append(swap(sent[-1]))

    margins = told[:, LANES:].reshape(size, slots)
    margins = jnp.sum(jnp.where(mine[:, None, None] == jnp.arange(slots, dtype=jnp.int32), margins, 0.0), axis=2)
    margins = margins.reshape(shards, 2, size)
    u, v = margins[:, 0, :, None], margins[:, 1, None, :]

    back = []
    for shard in range(shards):
        parts = scaled_parts(got[shard], counts, u, v, shard, steps)
        back.append(swap(grads(parts, pos, steps)))
    placed = [place(named, back[shard], shard, slots) for shard in range(shards - 1)]
    return tuple(update(named, back[-1], shards - 1, placed, row_table, col_table, row_accum, col_accum))


def solution(mesh):
    spec = P("dev", None, None)
    flat = P("dev", None)
    return jax.shard_map(
        functools.partial(body, devices=mesh.shape["dev"]),
        mesh=mesh,
        in_specs=(spec, spec, spec, spec, flat, flat, P("dev"), P("dev"), P(), spec),
        out_specs=(spec, spec, spec, spec),
        check_vma=False,
    )
```
